128 devices in a mesh: dp: 8 (over z, core), mp: 16 (over x, y).
Axes of the slice: x: 4, y: 4, z: 4, core: 2. Of those that a mesh axis runs over, the one named last changes fastest.
Arguments:
- grad_parts: bfloat16 [8, 2560, 128, 128], P('dp', 'mp'), may hold values from -6 to 6
- master: float32 [2560, 128, 128], P(('mp', 'dp')), may hold values from -0.018 to 0.018
- moment_first: float32 [2560, 128, 128], P(('mp', 'dp')), may hold values from -2 to 2
- moment_second: float32 [2560, 128, 128], P(('mp', 'dp')), may hold values from 0.02 to 1
- serving: bfloat16 [5120, 8192], P(None, 'mp'), may hold values from -0.017944336 to 0.017944336
- changed: int32 [2560], P(('mp', 'dp')), may hold values from 0 to 1, as said below
- hidden_pool: bfloat16 [1024, 5120], P(None, 'mp'), may hold values from -6 to 6
- row_ids: int32 [128], P('dp'), may hold values from 0 to 1023
- head_gain: float32 [128], replicated, may hold values from 0.5 to 1.5
Outputs:
- master_new: float32 [2560, 128, 128], P(('mp', 'dp'))
- first_new: float32 [2560, 128, 128], P(('mp', 'dp'))
- second_new: float32 [2560, 128, 128], P(('mp', 'dp'))
- serving_new: bfloat16 [5120, 8192], P(None, 'mp')
- scores: bfloat16 [128, 8192], P('dp', 'mp')
The draws below stay inside these ranges and needn't reach their ends.
Inputs may be any that keep to these rules, and one draw needn't show every extreme that they name: `changed`: in every draw all blocks of some run of 20 consecutive entries of the block order, run k being entries k * 20 to k * 20 + 19, are 1.
All inputs are finite; a program needn't handle non-finite values.
Results may differ from the reference program's by a relative error of at most 0.013.
Values may be sent and summed in bfloat16 or wider, within the bound.
No kernel may reach another device: no remote copies, remote signals or barrier semaphores. Data moves between devices by JAX's collectives and lax.ppermute only.
A program may use at most 128 MiB of HBM per device.

```python
import math
import jax
import jax.numpy as jnp
from jax import lax

D = 5120
HEADS = 64
HD = 128
H = 8192
BLK = 128
DB = 40
HB = 64
NBLK = 2560
BPO = 20
BW = 4
ROWS = 128
POOL = 1024
N_DP = 8
N_MP = 16


def draw_changed(key, part):
    key = jax.random.fold_in(key, 7)
    key_level, key_roll, key_run = jax.random.split(key, 3)
    position = jnp.arange(NBLK, dtype=jnp.int32)
    group = position % HB % (HB // BW)
    level = jax.random.randint(key_level, (HB // BW,), 2, 5)
    roll = jax.random.randint(key_roll, (NBLK,), 0, 4)
    keep = roll < level[group]
    full_run = jax.random.randint(key_run, (), 0, NBLK // BPO)
    keep = keep | (position // BPO == full_run)
    return keep.astype(jnp.int32)


def plant(drawn, stream_key, least, largest):
    place = [jax.random.randint(jax.random.fold_in(stream_key, axis), (), 0, length) for axis, length in enumerate(drawn.shape)]
    main_axis = drawn.shape.index(max(drawn.shape))
    beside = place[:main_axis] + [(place[main_axis] + 1) % drawn.shape[main_axis]] + place[main_axis + 1:]
    return drawn.at[tuple(place)].set(least).at[tuple(beside)].set(largest)


def with_spikes(drawn, key, source, target, shards_of, factor):
    owner, partner = [(jnp.arange(drawn.shape[dim]) // (drawn.shape[dim] // shards_of)).reshape([-1 if axis == dim else 1 for axis in range(drawn.ndim)]) for dim in (source, target)]
    chosen = jax.random.permutation(key, shards_of)[partner]
    strong = (owner == chosen) | (owner == (partner + shards_of // 2) % shards_of)
    return jnp.where(strong, factor * drawn, drawn)


def levels(key, extent, cuts, low, top_value):
    loudness = 1.0
    for dim, parts in cuts:
        heights = jax.random.uniform(jax.random.fold_in(jax.random.fold_in(key, 6), dim), (parts,), jnp.float32, low / len(cuts), top_value / len(cuts))
        loudness = loudness * jnp.repeat(jnp.exp(heights), extent[dim] // parts).reshape((-1,) + (1,) * (len(extent) - 1 - dim))
    return loudness


def noise(stream_key, extent, spread, most, cuts=(), held_as=jnp.bfloat16):
    result = jax.random.normal(stream_key, extent, jnp.float32) * spread
    if len(cuts) > 0:
        result = levels(stream_key, extent, cuts, -0.22, 0.18) * result
    return jnp.clip(result, min=-most, max=most).astype(held_as)


def gaussian_with(own_key, extent, deviation, limit, shards, heavy, kind=jnp.bfloat16):
    entries = deviation * jax.random.normal(own_key, extent, jnp.float32)
    if shards:
        entries = entries * levels(own_key, extent, shards, -0.22, 0.18)
    return jnp.clip(with_spikes(entries, jax.random.fold_in(own_key, 3), *heavy), -limit, limit).astype(kind)


def setup_inputs(seed: int = 0) -> dict:
    splits = jax.random.split(jax.random.key(seed), 10)
    return {
        "grad_parts": gaussian_with(splits[0], (N_DP, NBLK, BLK, BLK), 1.0, 6.0, ((0, 8), (1, 16)), (0, 1, 8, 2.0)),
        "master": noise(splits[1], (NBLK, BLK, BLK), 0.003, 0.018, ((0, 128),), jnp.float32),
        "moment_first": noise(splits[2], (NBLK, BLK, BLK), 0.3, 2.0, ((0, 128),), jnp.float32),
        "moment_second": jnp.clip(jnp.exp(math.log(1.0) - 3.912023 * jax.random.uniform(splits[3], (NBLK, BLK, BLK), jnp.float32) ** levels(splits[3], (NBLK, BLK, BLK), ((0, 128),), -0.2, 0.2)), 0.02, 1.0),
        "serving": noise(splits[4], (D, H), 0.003, 0.017944336, ((1, 16),)),
        "changed": draw_changed(jax.random.fold_in(splits[9], 71), 0),
        "hidden_pool": noise(splits[6], (POOL, D), 1.0, 6.0, ((1, 16),)),
        "row_ids": plant(jax.random.randint(splits[7], (ROWS,), 0, POOL), jax.random.fold_in(splits[7], 1), 0, POOL - 1).astype(jnp.int32),
        "head_gain": jnp.clip(1.0 + 0.1 * jax.random.normal(splits[8], (HD,), jnp.float32), 0.5, 1.5),
    }


beta_one = 0.9
beta_two = 0.999
correct_one = 1.0 - (0.9 ** 10) ** 10
correct_two = 1.0 - (0.999 ** 10) ** 10
adam_eps = 1e-08
learn_rate = 0.001
weight_decay = 0.1

def adam_update(gradient, master, moment_first, moment_second):
    first_new = beta_one * moment_first + (1.0 - beta_one) * gradient
    second_new = beta_two * moment_second + (1.0 - beta_two) * gradient * gradient
    update = first_new / correct_one / (jnp.sqrt(second_new / correct_two) + adam_eps) + weight_decay * master
    return (master - learn_rate * update, first_new, second_new)

def reference(grad_parts, master, moment_first, moment_second, serving, changed, hidden_pool, row_ids, head_gain):
    gradient = lax.optimization_barrier(jnp.sum(grad_parts, axis=0, dtype=jnp.float32))
    master_new, first_new, second_new = adam_update(gradient, master, moment_first, moment_second)
    fresh = master_new.astype(jnp.bfloat16)
    grid = fresh.reshape(DB, BW, N_MP, BLK, BLK).transpose(0, 3, 2, 1, 4)
    marked = changed.reshape(DB, BW, N_MP).transpose(0, 2, 1)[:, None, :, :, None] == 1
    current = serving.reshape(DB, BLK, N_MP, BW, BLK)
    serving_new = jnp.where(marked, grid, current).reshape(D, H)
    features = hidden_pool[row_ids]
    query = jnp.dot(features, serving_new, preferred_element_type=jnp.float32)
    heads = query.reshape(ROWS, HEADS, HD)
    normed = heads * lax.rsqrt(lax.optimization_barrier(jnp.mean(heads * heads, axis=-1, keepdims=True)) + 1e-06) * head_gain
    scores = normed.reshape(ROWS, H).astype(jnp.bfloat16)
    return (master_new, first_new, second_new, serving_new, scores)
```

```python
import functools

import jax
import jax.numpy as jnp
from jax import lax
from jax.experimental import pallas as pl
from jax.experimental.pallas import tpu as pltpu
from jax.sharding import PartitionSpec as P

beta_one = 0.9
beta_two = 0.999
correct_one = 1.0 - (0.9**10) ** 10
correct_two = 1.0 - (0.999**10) ** 10
adam_eps = 1e-08
learn_rate = 0.001
weight_decay = 0.1

f32 = jnp.float32
bf16 = jnp.bfloat16
MiB = 1024 * 1024

Z_UP = [(i, (i + 2) % 8) for i in range(8)]
Z_DOWN = [(i, (i - 2) % 8) for i in range(8)]
CORE = [(i, i ^ 1) for i in range(8)]
SWAP = [
    (d * 16 + x * 4 + y, (d // 4 * 4 + x) * 16 + (d % 4) * 4 + y)
    for d in range(8)
    for x in range(4)
    for y in range(4)
]


def along_x(s):
    return [(x * 4 + y, (x + s) % 4 * 4 + y) for x in range(4) for y in range(4)]


def along_y(s):
    return [(x * 4 + y, x * 4 + (y + s) % 4) for x in range(4) for y in range(4)]


def on_dp(value, pairs):
    return lax.ppermute(value, "dp", pairs)


def on_mp(value, pairs):
    return lax.ppermute(value, "mp", pairs)


def add(a, b):
    return (a.astype(f32) + b.astype(f32)).astype(bf16)


def adam_kernel(
    place,
    marked,
    own,
    other,
    below_a,
    below_b,
    above_a,
    above_b,
    master,
    first,
    second,
    master_out,
    first_out,
    second_out,
    *slots,
):
    step = pl.program_id(0)
    x, y, e = place[1], place[2], place[3]
    slot = jnp.where(step == 4, 4, (step + e - x + 4) % 4)
    for block in range(4):
        halves = []
        for rows, below, above in (
            (pl.ds(0, 64), below_a, above_a),
            (pl.ds(64, 64), below_b, above_b),
        ):
            gradient = (
                own[0, block, rows].astype(f32)
                + other[block, rows].astype(f32)
                + below[block].astype(f32)
                + above[block].astype(f32)
            )
            weight = master[block, rows]
            first_new = beta_one * first[block, rows] + (1.0 - beta_one) * gradient
            second_new = (
                beta_two * second[block, rows] + (1.0 - beta_two) * gradient * gradient
            )
            update = (
                first_new / correct_one / (jnp.sqrt(second_new / correct_two) + adam_eps)
                + weight_decay * weight
            )
            weight_new = weight - learn_rate * update
            master_out[block, rows] = weight_new
            first_out[block, rows] = first_new
            second_out[block, rows] = second_new
            halves.append(weight_new)
        flag = marked[step * 4 + block]
        fresh = jnp.concatenate(halves, axis=0)
        fresh = jnp.where(flag == 1, fresh, jnp.inf).astype(bf16)
        at = (block - y + 4) % 4
        for i in range(5):

            @pl.when(slot == i)
            def _():
                slots[i][at] = fresh


def adam(place, changed, grad_parts, other, below_a, below_b, above_a, above_b, *state):
    def rows(height):
        return pl.BlockSpec((4, height, 128), lambda i, place, marked: (i, 0, 0))

    own = pl.BlockSpec((1, 4, 128, 128), lambda i, place, marked: (0, place[0] * 5 + i, 0, 0))
    whole = pl.BlockSpec((4, 128, 128), lambda i, place, marked: (0, 0, 0))
    return pl.pallas_call(
        adam_kernel,
        grid_spec=pltpu.PrefetchScalarGridSpec(
            num_scalar_prefetch=2,
            grid=(5,),
            in_specs=[own, rows(128)] + [rows(64)] * 4 + [rows(128)] * 3,
            out_specs=[rows(128)] * 3 + [whole] * 5,
        ),
        out_shape=[jax.ShapeDtypeStruct((20, 128, 128), f32)] * 3
        + [jax.ShapeDtypeStruct((4, 128, 128), bf16)] * 5,
        compiler_params=pltpu.CompilerParams(vmem_limit_bytes=32 * MiB),
        cost_estimate=pl.CostEstimate(
            flops=20 * 128 * 128 * 20, bytes_accessed=11 * MiB, transcendentals=2 * 20 * 128 * 128
        ),
    )(place, changed, grad_parts, other, below_a, below_b, above_a, above_b, *state)


def place_kernel(place, serving, features, gain, *refs):
    pieces, out, scores = refs[:16], refs[16], refs[17]
    x, y, z, core = place[1], place[2], place[4], place[5]
    for number in range(16):
        k, q, h = number // 4, number // 2 % 2, number % 2
        piece = pieces[number]
        z_from = (z + k) % 4
        core_from = core ^ q
        e_from = 2 * (z_from % 2) + core_from
        base = 5 * (z_from // 2)

        def put(u, carry):
            y_from = (y - (2 * h + u) + 4) % 4
            for s in range(5):
                if s < 4:
                    x_from = (x - s + 4) % 4
                    t = 10 * (4 * x_from + y_from) + base + e_from + (e_from > x).astype(jnp.int32)
                else:
                    t = 10 * (4 * e_from + y_from) + base + x + 1
                rows = pl.ds(pl.multiple_of(t // 4 * 128, 128), 128)
                columns = pl.ds(pl.multiple_of(t % 4 * 128, 128), 128)
                block = piece[u * 5 + s]
                held = serving[rows, columns]
                out[rows, columns] = jnp.where(block.astype(f32) == jnp.inf, held, block)
            return carry

        lax.fori_loop(0, 2, put, 0)

    total = jnp.zeros((16, 512), f32)
    for u in range(4):
        for s in range(4):
            x_from = (x - s + 4) % 4
            y_from = (y - u + 4) % 4
            rows = pl.ds(pl.multiple_of((4 * x_from + y_from) * 320, 64), 320)
            total += jnp.dot(features[u * 4 + s], out[rows, :], preferred_element_type=f32)
    for head in range(4):
        query = total[:, head * 128 : head * 128 + 128]
        scale = lax.rsqrt(jnp.mean(query * query, axis=-1, keepdims=True) + 1e-06)
        scores[:, head * 128 : head * 128 + 128] = (query * scale * gain[...]).astype(bf16)


def put_and_score(place, serving, features, gain, pieces):
    vmem = pl.BlockSpec(memory_space=pltpu.VMEM)
    return pl.pallas_call(
        place_kernel,
        in_specs=[pl.BlockSpec(memory_space=pltpu.SMEM)] + [vmem] * 19,
        out_specs=[vmem] * 2,
        out_shape=[
            jax.ShapeDtypeStruct((5120, 512), bf16),
            jax.ShapeDtypeStruct((16, 512), bf16),
        ],
        compiler_params=pltpu.CompilerParams(vmem_limit_bytes=48 * MiB),
        cost_estimate=pl.CostEstimate(
            flops=2 * 16 * 5120 * 512, bytes_accessed=16 * MiB, transcendentals=0
        ),
    )(place, serving, features, gain, *pieces)


def on_device(
    grad_parts,
    master,
    moment_first,
    moment_second,
    serving,
    changed,
    hidden_pool,
    row_ids,
    head_gain,
):
    dp = lax.axis_index("dp")
    mp = lax.axis_index("mp")
    z, core = dp // 2, dp % 2
    x, y = mp // 4, mp % 4
    place = jnp.stack([dp, x, y, dp % 4, z, core]).astype(jnp.int32)

    picked = jnp.take(hidden_pool, row_ids, axis=0, mode="clip")
    row = jnp.stack([picked] + [on_mp(picked, along_x(s)) for s in (1, 2, 3)])
    features = jnp.concatenate([row] + [on_mp(row, along_y(s)) for s in (1, 2, 3)])

    parts = grad_parts.reshape(4, 2, 20, 128, 128)

    def part(k, c):
        start = ((z + k) % 4, c, 0, 0, 0)
        return lax.dynamic_slice(parts, start, (1, 1, 20, 128, 128))[0, 0]

    sums = {}
    for k in (2, 1, 3):
        sums[k] = add(part(k, core), on_dp(part(k, 1 - core), CORE))
    far_a = on_dp(sums[2][:, :64], Z_UP)
    far_b = on_dp(sums[2][:, 64:], Z_DOWN)
    below_b = on_dp(sums[1][:, 64:], Z_UP)
    above_a = on_dp(sums[3][:, :64], Z_DOWN)
    other = on_dp(part(0, 1 - core), CORE)
    below_a = on_dp(add(sums[1][:, :64], far_a), Z_UP)
    above_b = on_dp(add(sums[3][:, 64:], far_b), Z_DOWN)

    master_new, first_new, second_new, *slots = adam(
        place,
        changed,
        grad_parts,
        other,
        below_a,
        below_b,
        above_a,
        above_b,
        master,
        moment_first,
        moment_second,
    )

    row = [slots[0]] + [on_mp(slots[s], along_x(s)) for s in (1, 2, 3)]
    row.append(lax.ppermute(slots[4], ("dp", "mp"), SWAP))
    plane = []
    for u in range(4):
        group = jnp.stack([r[u] for r in row])
        plane.append(on_mp(group, along_y(u)) if u else group)

    a = jnp.concatenate(plane[:2])
    b = jnp.concatenate(plane[2:])
    below_a = on_dp(a, Z_UP)
    above_b = on_dp(b, Z_DOWN)
    below_b = on_dp(b, Z_UP)
    above_a = on_dp(a, Z_DOWN)
    far_a = on_dp(below_a, Z_UP)
    far_b = on_dp(above_b, Z_DOWN)
    pieces = []
    for pair in ((a, b), (above_a, above_b), (far_a, far_b), (below_a, below_b)):
        pieces += list(pair) + [on_dp(value, CORE) for value in pair]

    serving_new, scores = put_and_score(
        place, serving, features, head_gain.reshape(1, 128), pieces
    )
    return (master_new, first_new, second_new, serving_new, scores)


def solution(mesh):
    return jax.shard_map(
        on_device,
        mesh=mesh,
        in_specs=(
            P("dp", "mp", None, None),
            P(("mp", "dp"), None, None),
            P(("mp", "dp"), None, None),
            P(("mp", "dp"), None, None),
            P(None, "mp"),
            P(("mp", "dp")),
            P(None, "mp"),
            P("dp"),
            P(),
        ),
        out_specs=(
            P(("mp", "dp"), None, None),
            P(("mp", "dp"), None, None),
            P(("mp", "dp"), None, None),
            P(None, "mp"),
            P("dp", "mp"),
        ),
        check_vma=False,
    )
```

```python
import functools

import jax
import jax.numpy as jnp
from jax import lax
from jax.experimental import pallas as pl
from jax.experimental.pallas import tpu as pltpu
from jax.sharding import PartitionSpec as P

beta_one = 0.9
beta_two = 0.999
correct_one = 1.0 - (0.9**10) ** 10
correct_two = 1.0 - (0.999**10) ** 10
adam_eps = 1e-08
learn_rate = 0.001
weight_decay = 0.1

f32 = jnp.float32
bf16 = jnp.bfloat16
MiB = 1024 * 1024

Z_WAY = [(2 * z + c, 2 * ((z + 1 - 2 * c) % 4) + c) for z in range(4) for c in range(2)]
Z_BACK = [(2 * z + c, 2 * ((z + 3 + 2 * c) % 4) + c) for z in range(4) for c in range(2)]
CORE = [(i, i ^ 1) for i in range(8)]
SWAP = [
    (d * 16 + x * 4 + y, (d // 4 * 4 + x) * 16 + (d % 4) * 4 + y)
    for d in range(8)
    for x in range(4)
    for y in range(4)
]


def along_x(s):
    return [(x * 4 + y, (x + s) % 4 * 4 + y) for x in range(4) for y in range(4)]


def along_y(s):
    return [(x * 4 + y, x * 4 + (y + s) % 4) for x in range(4) for y in range(4)]


def on_dp(value, pairs):
    return lax.ppermute(value, "dp", pairs)


def on_mp(value, pairs):
    return lax.ppermute(value, "mp", pairs)


VMEM = pl.BlockSpec(memory_space=pltpu.VMEM)
SMEM = pl.BlockSpec(memory_space=pltpu.SMEM)
ANY = pl.BlockSpec(memory_space=pl.ANY)
BRIEF = pl.CostEstimate(flops=1000, bytes_accessed=1000, transcendentals=0)


def add(*terms):
    return sum(term.astype(f32) for term in terms).astype(bf16)


def tie(value, *earlier):
    return pl.pallas_call(
        lambda *refs: None,
        in_specs=[ANY] * (1 + len(earlier)),
        out_specs=ANY,
        out_shape=jax.ShapeDtypeStruct(value.shape, value.dtype),
        input_output_aliases={0: 0},
        compiler_params=pltpu.CompilerParams(vmem_limit_bytes=MiB),
        cost_estimate=BRIEF,
    )(value, *earlier)


def adam_kernel(place, marked, picked, near, relay, master, first, second, *refs):
    outs, slots = refs[:3], refs[3:]
    step = pl.program_id(0)
    x, y, e = place[1], place[2], place[3]
    to = jnp.where(step == 4, 4, (step + e - x + 4) % 4)
    for block in range(4):
        gradient = near[block] + relay[block].astype(f32)
        weight = master[block]
        first_new = beta_one * first[block] + (1.0 - beta_one) * gradient
        second_new = beta_two * second[block] + (1.0 - beta_two) * gradient * gradient
        update = (
            first_new / correct_one / (jnp.sqrt(second_new / correct_two) + adam_eps)
            + weight_decay * weight
        )
        weight_new = weight - learn_rate * update
        outs[0][block] = weight_new
        outs[1][block] = first_new
        outs[2][block] = second_new
        flag = marked[step * 4 + block]
        fresh = jnp.where(flag == 1, weight_new, jnp.inf).astype(bf16)
        rows = pl.ds(pl.multiple_of((block - y + 4) % 4 * 128, 128), 128)
        for number, slot in enumerate(slots):

            @pl.when(to == number)
            def _():
                slot[rows, :] = fresh

    @pl.when(step == 0)
    def _():
        for slot in slots[:4]:
            for j in range(3):
                slot[512 + 16 * j : 528 + 16 * j, :] = picked[:, 128 * j : 128 * j + 128]


def adam(place, changed, picked, terms, state):
    rows = pl.BlockSpec((4, 128, 128), lambda i, place, marked: (i, 0, 0))

    def whole(height, width):
        return pl.BlockSpec((height, width), lambda i, place, marked: (0, 0))

    heights = (560, 560, 560, 560, 512)
    return pl.pallas_call(
        adam_kernel,
        grid_spec=pltpu.PrefetchScalarGridSpec(
            num_scalar_prefetch=2,
            grid=(5,),
            in_specs=[whole(16, 384)] + [rows] * 5,
            out_specs=[rows] * 3 + [whole(height, 128) for height in heights],
        ),
        out_shape=[jax.ShapeDtypeStruct((20, 128, 128), f32)] * 3
        + [jax.ShapeDtypeStruct((height, 128), bf16) for height in heights],
        compiler_params=pltpu.CompilerParams(vmem_limit_bytes=16 * MiB),
        cost_estimate=BRIEF,
    )(place, changed, picked, *terms, *state)


def origin(place, steps, crossed, u, s):
    x, y, z, core = place[1], place[2], place[4], place[5]
    z_from = (z + steps * (1 - 2 * core) + 4) % 4
    e_from = 2 * (z_from % 2) + (core ^ crossed)
    y_from = (y - u + 4) % 4
    x_from = (x - s + 4) % 4
    late = (e_from > x).astype(jnp.int32)
    t = jnp.where(
        s < 4,
        10 * (4 * x_from + y_from) + e_from + late,
        10 * (4 * e_from + y_from) + x + 1,
    )
    t = t + 5 * (z_from // 2)
    return t // 4, t % 4


def blocks(place, where_from, pieces, body):
    for number, (piece, (steps, crossed)) in enumerate(zip(pieces, where_from)):

        def group(u, carry):
            for s in range(5):
                row, column = origin(place, steps, crossed, u, s)
                i = u * 5 + s
                body(number * 20 + i, None if piece is None else piece[i], row, column)
            return carry

        lax.fori_loop(0, 4, group, 0)


def spot(row, column):
    rows = pl.ds(pl.multiple_of(row * 128, 128), 128)
    return rows, pl.ds(pl.multiple_of(column * 128, 128), 128)


FIRST = ((0, 0), (0, 1))
SECOND = ((-1, 0), (1, 1), (-1, 1), (1, 0))
LAST = ((2, 0), (2, 1))


def first_kernel(place, serving, mine, paired, out, old, sem):
    copy = pltpu.make_async_copy(serving, out, sem)
    copy.start()
    copy.wait()

    def put(i, block, row, column):
        at = spot(row, column)
        out[at] = jnp.where(block == jnp.inf, out[at], block)

    def keep(i, block, row, column):
        at = spot(row, column)
        old[i] = out[at]
        out[at] = jnp.zeros((128, 128), bf16)

    blocks(place, FIRST, (mine, paired), put)
    blocks(place, LAST, (None, None), keep)


def second_kernel(place, picked, *refs):
    pieces, (_, work, out, total, features, sems) = refs[:4], refs[4:]
    features[...] = jnp.zeros((40, 16, 128), bf16)
    for u in range(4):
        for s in range(4):
            at = 4 * ((place[1] - s + 4) % 4) + (place[2] - u + 4) % 4
            tile = 5 * (at // 2) + 2 * (at % 2)
            for j in range(3):
                features[tile + j] += picked[u, pl.ds(s * 48 + j * 16, 16), :]

    def put(i, block, row, column):
        at = spot(row, column)
        work[at] = jnp.where(block == jnp.inf, work[at], block)

    def write(i):
        rows = pl.ds(i * 640, 640)
        return pltpu.make_async_copy(work.at[rows], out.at[rows], sems.at[i])

    blocks(place, SECOND, pieces, put)
    for i in range(8):
        write(i).start()
    query = jnp.zeros((16, 512), f32)
    for i in range(8):
        left = jnp.concatenate([features[5 * i + j] for j in range(5)], axis=1)
        query += jnp.dot(left, work[640 * i : 640 * i + 640, :], preferred_element_type=f32)
    for column in range(4):
        total[column] = query[:, column * 128 : column * 128 + 128]
    for i in range(8):
        write(i).wait()


def last_kernel(
    place, features, gain, before, old, piece, crossed, _, out, scores, total, held, sems
):
    total[...] = before[...]
    writes = []
    for number, (source, (steps, cross)) in enumerate(zip((piece, crossed), LAST)):
        for odd in range(2):
            for wanted in ((0, 1, 2, 3), (4,)):
                first = len(writes)
                left = []
                for s in wanted:
                    for u in (odd, odd + 2):
                        row, column = origin(place, steps, cross, u, s)
                        i, n = u * 5 + s, len(writes)
                        block = source[i]
                        held[n] = jnp.where(block == jnp.inf, old[number * 20 + i], block)
                        to = out.at[spot(row, column)]
                        writes.append(pltpu.make_async_copy(held.at[n], to, sems.at[n]))
                        writes[n].start()
                        left.append(features[row])
                right = held[first : len(writes)].reshape(-1, 128)
                left = jnp.concatenate(left, axis=1)
                total[column] += jnp.dot(left, right, preferred_element_type=f32)
    for head in range(4):
        query = total[head]
        scale = lax.rsqrt(jnp.mean(query * query, axis=-1, keepdims=True) + 1e-06)
        scores[:, head * 128 : head * 128 + 128] = (query * scale * gain[...]).astype(bf16)
    for write in writes:
        write.wait()


SERVING = jax.ShapeDtypeStruct((5120, 512), bf16)
OLD = jax.ShapeDtypeStruct((40, 128, 128), bf16)
FEATURES = jax.ShapeDtypeStruct((40, 16, 128), bf16)
TOTAL = jax.ShapeDtypeStruct((4, 16, 128), f32)
SCORES = jax.ShapeDtypeStruct((16, 512), bf16)


def local(kernel, in_specs, out_specs, out_shape, scratch=(), aliases={}):
    return pl.pallas_call(
        kernel,
        in_specs=in_specs,
        out_specs=out_specs,
        out_shape=out_shape,
        scratch_shapes=scratch,
        input_output_aliases=aliases,
        compiler_params=pltpu.CompilerParams(vmem_limit_bytes=16 * MiB),
        cost_estimate=BRIEF,
    )


def on_device(
    grad_parts,
    master,
    moment_first,
    moment_second,
    serving,
    changed,
    hidden_pool,
    row_ids,
    head_gain,
):
    dp = lax.axis_index("dp")
    mp = lax.axis_index("mp")
    z, core = dp // 2, dp % 2
    x, y = mp // 4, mp % 4
    place = jnp.stack([dp, x, y, dp % 4, z, core]).astype(jnp.int32)

    other = 1 - core
    up = (z + 5 - 2 * core) % 4
    down = (z + 3 + 2 * core) % 4
    opposite = (z + 2) % 4

    picked = jnp.take(hidden_pool, row_ids, axis=0, mode="clip")
    even, odd = (jnp.pad(picked, ((0, 0), ends)) for ends in ((0, 64), (64, 0)))
    picked = jnp.where(y % 2 == 1, odd, even)

    parts = grad_parts.reshape(4, 2, 20, 128, 128)

    def part(chip, c, at=0, count=20):
        start = (chip, c, at, 0, 0)
        return lax.dynamic_slice(parts, start, (1, 1, count, 128, 128))[0, 0]

    def after(*values):
        nonlocal parts
        parts, *values = lax.optimization_barrier((parts, *values))
        return values

    far_out, far_keep = part(opposite, other), part(opposite, core)
    (far_out,) = after(far_out)
    direct_out, relay_out = part(up, other), part(down, other)
    far_in = tie(on_dp(far_out, CORE), direct_out, relay_out)
    (far,) = after(add(far_keep, far_in))
    far = on_dp(far, Z_WAY)
    direct_in = tie(on_dp(direct_out, CORE), picked)
    (direct,) = after(add(part(down, core), direct_in))
    (relay,) = after(add(part(up, core), on_dp(relay_out, CORE)))
    far = tie(far, direct, relay)
    direct = on_dp(direct, Z_BACK)
    relay = on_dp(add(relay, far), Z_WAY)
    own, own_out = after(part(z, core), part(z, other))
    near = own.astype(f32) + on_dp(own_out, CORE).astype(f32) + direct.astype(f32)

    state = (master, moment_first, moment_second)
    *state_new, row0, row1, row2, row3, extra = adam(
        place, changed, picked, (near, relay), state
    )

    extra = lax.ppermute(extra, ("dp", "mp"), SWAP)
    row = [row0] + [on_mp(r, along_x(s)) for s, r in ((1, row1), (2, row2), (3, row3))]
    plane, features = [], []
    for u in range(4):
        group = [r[128 * u : 128 * u + 128] for r in row + [extra]]
        group = jnp.concatenate(group + [r[512:] for r in row])
        if u:
            group = on_mp(group, along_y(u))
        plane.append(group[:640])
        features.append(group[640:])
    features = jnp.stack(features)
    mine = jnp.concatenate(plane).reshape(20, 128, 128)

    near = on_dp(mine, Z_WAY)
    paired = on_dp(mine, CORE)
    near_paired = on_dp(paired, Z_WAY)

    work, old = local(
        first_kernel,
        [SMEM, ANY, VMEM, VMEM],
        [VMEM] * 2,
        [SERVING, OLD],
        [pltpu.SemaphoreType.DMA(())],
    )(place, serving, mine, paired)
    near = tie(near, old)
    far = on_dp(near, Z_WAY)
    pieces = (near, on_dp(near, CORE), near_paired, on_dp(near_paired, CORE))
    _, out, total, features = local(
        second_kernel,
        [SMEM] + [VMEM] * 6,
        [VMEM, ANY, VMEM, VMEM],
        [SERVING, SERVING, TOTAL, FEATURES],
        [pltpu.SemaphoreType.DMA((8,))],
        {6: 0},
    )(place, features, *pieces, work)
    far = tie(far, total)
    serving_new, scores = local(
        last_kernel,
        [SMEM] + [VMEM] * 6 + [ANY],
        [ANY, VMEM],
        [SERVING, SCORES],
        [
            pltpu.VMEM(TOTAL.shape, f32),
            pltpu.VMEM(OLD.shape, bf16),
            pltpu.SemaphoreType.DMA((40,)),
        ],
        {7: 0},
    )(
        place,
        features,
        head_gain.reshape(1, 128),
        total,
        old,
        far,
        on_dp(far, CORE),
        out,
    )
    return (*state_new, serving_new, scores)


def solution(mesh):
    return jax.shard_map(
        on_device,
        mesh=mesh,
        in_specs=(
            P("dp", "mp", None, None),
            P(("mp", "dp"), None, None),
            P(("mp", "dp"), None, None),
            P(("mp", "dp"), None, None),
            P(None, "mp"),
            P(("mp", "dp")),
            P(None, "mp"),
            P("dp"),
            P(),
        ),
        out_specs=(
            P(("mp", "dp"), None, None),
            P(("mp", "dp"), None, None),
            P(("mp", "dp"), None, None),
            P(None, "mp"),
            P("dp", "mp"),
        ),
        check_vma=False,
    )
```

```python
import functools

import jax
import jax.numpy as jnp
from jax import lax
from jax.experimental import pallas as pl
from jax.experimental.pallas import tpu as pltpu
from jax.sharding import PartitionSpec as P

beta_one = 0.9
beta_two = 0.999
correct_one = 1.0 - (0.9**10) ** 10
correct_two = 1.0 - (0.999**10) ** 10
adam_eps = 1e-08
learn_rate = 0.001
weight_decay = 0.1

f32 = jnp.float32
bf16 = jnp.bfloat16
MiB = 1024 * 1024

Z_WAY = [(2 * z + c, 2 * ((z + 1 - 2 * c) % 4) + c) for z in range(4) for c in range(2)]
Z_BACK = [(2 * z + c, 2 * ((z + 3 + 2 * c) % 4) + c) for z in range(4) for c in range(2)]
CORE = [(i, i ^ 1) for i in range(8)]
SWAP = [
    (d * 16 + x * 4 + y, (d // 4 * 4 + x) * 16 + (d % 4) * 4 + y)
    for d in range(8)
    for x in range(4)
    for y in range(4)
]


def along_x(s):
    return [(x * 4 + y, (x + s) % 4 * 4 + y) for x in range(4) for y in range(4)]


def along_y(s):
    return [(x * 4 + y, x * 4 + (y + s) % 4) for x in range(4) for y in range(4)]


def on_dp(value, pairs):
    return lax.ppermute(value, "dp", pairs)


def on_mp(value, pairs):
    return lax.ppermute(value, "mp", pairs)


VMEM = pl.BlockSpec(memory_space=pltpu.VMEM)
SMEM = pl.BlockSpec(memory_space=pltpu.SMEM)
ANY = pl.BlockSpec(memory_space=pl.ANY)
BRIEF = pl.CostEstimate(flops=1000, bytes_accessed=1000, transcendentals=0)


def add(*terms):
    return sum(term.astype(f32) for term in terms).astype(bf16)


def tie(value, *earlier):
    return pl.pallas_call(
        lambda *refs: None,
        in_specs=[ANY] * (1 + len(earlier)),
        out_specs=ANY,
        out_shape=jax.ShapeDtypeStruct(value.shape, value.dtype),
        input_output_aliases={0: 0},
        compiler_params=pltpu.CompilerParams(vmem_limit_bytes=MiB),
        cost_estimate=BRIEF,
    )(value, *earlier)


def adam_kernel(place, marked, picked, near, relay, master, first, second, *refs):
    outs, slots = refs[:3], refs[3:]
    step = pl.program_id(0)
    x, y, e = place[1], place[2], place[3]
    to = jnp.where(step == 4, 4, (step + e - x + 4) % 4)
    for block in range(4):
        gradient = near[block] + relay[block].astype(f32)
        weight = master[block]
        first_new = beta_one * first[block] + (1.0 - beta_one) * gradient
        second_new = beta_two * second[block] + (1.0 - beta_two) * gradient * gradient
        update = (
            first_new / correct_one / (jnp.sqrt(second_new / correct_two) + adam_eps)
            + weight_decay * weight
        )
        weight_new = weight - learn_rate * update
        outs[0][block] = weight_new
        outs[1][block] = first_new
        outs[2][block] = second_new
        flag = marked[step * 4 + block]
        fresh = jnp.where(flag == 1, weight_new, jnp.inf).astype(bf16)
        rows = pl.ds(pl.multiple_of((block - y + 4) % 4 * 128, 128), 128)
        for number, slot in enumerate(slots):

            @pl.when(to == number)
            def _():
                slot[rows, :] = fresh

    @pl.when(step == 0)
    def _():
        for slot in slots[:4]:
            for j in range(3):
                slot[512 + 16 * j : 528 + 16 * j, :] = picked[:, 128 * j : 128 * j + 128]


def adam(place, changed, picked, terms, state):
    rows = pl.BlockSpec((4, 128, 128), lambda i, place, marked: (i, 0, 0))

    def whole(height, width):
        return pl.BlockSpec((height, width), lambda i, place, marked: (0, 0))

    heights = (560, 560, 560, 560, 512)
    return pl.pallas_call(
        adam_kernel,
        grid_spec=pltpu.PrefetchScalarGridSpec(
            num_scalar_prefetch=2,
            grid=(5,),
            in_specs=[whole(16, 384)] + [rows] * 5,
            out_specs=[rows] * 3 + [whole(height, 128) for height in heights],
        ),
        out_shape=[jax.ShapeDtypeStruct((20, 128, 128), f32)] * 3
        + [jax.ShapeDtypeStruct((height, 128), bf16) for height in heights],
        compiler_params=pltpu.CompilerParams(vmem_limit_bytes=16 * MiB),
        cost_estimate=BRIEF,
    )(place, changed, picked, *terms, *state)


def origin(place, steps, crossed, u, s):
    x, y, z, core = place[1], place[2], place[4], place[5]
    z_from = (z + steps * (1 - 2 * core) + 4) % 4
    e_from = 2 * (z_from % 2) + (core ^ crossed)
    y_from = (y - u + 4) % 4
    x_from = (x - s + 4) % 4
    late = (e_from > x).astype(jnp.int32)
    t = jnp.where(
        s < 4,
        10 * (4 * x_from + y_from) + e_from + late,
        10 * (4 * e_from + y_from) + x + 1,
    )
    t = t + 5 * (z_from // 2)
    return t // 4, t % 4


def blocks(place, where_from, pieces, body):
    for number, (piece, (steps, crossed)) in enumerate(zip(pieces, where_from)):

        def group(u, carry):
            for s in range(5):
                row, column = origin(place, steps, crossed, u, s)
                i = u * 5 + s
                body(number * 20 + i, None if piece is None else piece[i], row, column)
            return carry

        lax.fori_loop(0, 4, group, 0)


def spot(row, column):
    rows = pl.ds(pl.multiple_of(row * 128, 128), 128)
    return rows, pl.ds(pl.multiple_of(column * 128, 128), 128)


FIRST = ((0, 0), (0, 1))
SECOND = ((-1, 0), (1, 1), (-1, 1), (1, 0))
LAST = ((2, 0), (2, 1))


def first_kernel(place, serving, mine, paired, out, old, sem):
    copy = pltpu.make_async_copy(serving, out, sem)
    copy.start()
    copy.wait()

    def put(i, block, row, column):
        at = spot(row, column)
        out[at] = jnp.where(block == jnp.inf, out[at], block)

    def keep(i, block, row, column):
        at = spot(row, column)
        old[i] = out[at]
        out[at] = jnp.zeros((128, 128), bf16)

    blocks(place, FIRST, (mine, paired), put)
    blocks(place, LAST, (None, None), keep)


def second_kernel(place, picked, *refs):
    pieces, (_, work, out, total, features, sems) = refs[:4], refs[4:]
    features[...] = jnp.zeros((40, 16, 128), bf16)
    for u in range(4):
        for s in range(4):
            at = 4 * ((place[1] - s + 4) % 4) + (place[2] - u + 4) % 4
            tile = 5 * (at // 2) + 2 * (at % 2)
            for j in range(3):
                features[tile + j] += picked[u, pl.ds(s * 48 + j * 16, 16), :]

    def put(i, block, row, column):
        at = spot(row, column)
        work[at] = jnp.where(block == jnp.inf, work[at], block)

    def write(i):
        rows = pl.ds(i * 640, 640)
        return pltpu.make_async_copy(work.at[rows], out.at[rows], sems.at[i])

    blocks(place, SECOND, pieces, put)
    for i in range(8):
        write(i).start()
    query = jnp.zeros((16, 512), f32)
    for i in range(8):
        left = jnp.concatenate([features[5 * i + j] for j in range(5)], axis=1)
        query += jnp.dot(left, work[640 * i : 640 * i + 640, :], preferred_element_type=f32)
    for column in range(4):
        total[column] = query[:, column * 128 : column * 128 + 128]
    for i in range(8):
        write(i).wait()


def last_kernel(
    place, features, gain, before, old, piece, crossed, _, out, scores, total, held, sems
):
    total[...] = before[...]
    writes = []
    for number, (source, (steps, cross)) in enumerate(zip((piece, crossed), LAST)):
        for odd in range(2):
            for wanted in ((0, 1, 2, 3), (4,)):
                first = len(writes)
                left = []
                for s in wanted:
                    for u in (odd, odd + 2):
                        row, column = origin(place, steps, cross, u, s)
                        i, n = u * 5 + s, len(writes)
                        block = source[i]
                        held[n] = jnp.where(block == jnp.inf, old[number * 20 + i], block)
                        to = out.at[spot(row, column)]
                        writes.append(pltpu.make_async_copy(held.at[n], to, sems.at[n]))
                        writes[n].start()
                        left.append(features[row])
                right = held[first : len(writes)].reshape(-1, 128)
                left = jnp.concatenate(left, axis=1)
                total[column] += jnp.dot(left, right, preferred_element_type=f32)
    for head in range(4):
        query = total[head]
        scale = lax.rsqrt(jnp.mean(query * query, axis=-1, keepdims=True) + 1e-06)
        scores[:, head * 128 : head * 128 + 128] = (query * scale * gain[...]).astype(bf16)
    for write in writes:
        write.wait()


SERVING = jax.ShapeDtypeStruct((5120, 512), bf16)
OLD = jax.ShapeDtypeStruct((40, 128, 128), bf16)
FEATURES = jax.ShapeDtypeStruct((40, 16, 128), bf16)
TOTAL = jax.ShapeDtypeStruct((4, 16, 128), f32)
SCORES = jax.ShapeDtypeStruct((16, 512), bf16)


def local(kernel, in_specs, out_specs, out_shape, scratch=(), aliases={}):
    return pl.pallas_call(
        kernel,
        in_specs=in_specs,
        out_specs=out_specs,
        out_shape=out_shape,
        scratch_shapes=scratch,
        input_output_aliases=aliases,
        compiler_params=pltpu.CompilerParams(vmem_limit_bytes=16 * MiB),
        cost_estimate=BRIEF,
    )


def on_device(
    grad_parts,
    master,
    moment_first,
    moment_second,
    serving,
    changed,
    hidden_pool,
    row_ids,
    head_gain,
):
    dp = lax.axis_index("dp")
    mp = lax.axis_index("mp")
    z, core = dp // 2, dp % 2
    x, y = mp // 4, mp % 4
    place = jnp.stack([dp, x, y, dp % 4, z, core]).astype(jnp.int32)

    other = 1 - core
    up = (z + 5 - 2 * core) % 4
    down = (z + 3 + 2 * core) % 4
    opposite = (z + 2) % 4

    picked = jnp.take(hidden_pool, row_ids, axis=0, mode="clip")
    even, odd = (jnp.pad(picked, ((0, 0), ends)) for ends in ((0, 64), (64, 0)))
    picked = jnp.where(y % 2 == 1, odd, even)

    parts = grad_parts.reshape(4, 2, 20, 128, 128)

    def part(chip, c, at=0, count=20):
        start = (chip, c, at, 0, 0)
        return lax.dynamic_slice(parts, start, (1, 1, count, 128, 128))[0, 0]

    def after(*values):
        nonlocal parts
        parts, *values = lax.optimization_barrier((parts, *values))
        return values

    far_out, far_keep = part(opposite, other), part(opposite, core)
    (far_out,) = after(far_out)
    direct_out, relay_out = part(up, other), part(down, other)
    (far,) = after(add(far_keep, on_dp(far_out, CORE)))
    far = on_dp(far, Z_WAY)
    (relay,) = after(add(part(up, core), on_dp(relay_out, CORE)))
    (own_out,) = after(part(z, other))
    direct_in = tie(on_dp(direct_out, CORE), relay, own_out)
    (direct,) = after(add(part(down, core), direct_in))
    far = tie(far, direct, picked)
    direct = on_dp(direct, Z_BACK)
    relay = on_dp(add(relay, far), Z_WAY)
    own = part(z, core).astype(f32) + on_dp(own_out, CORE).astype(f32)
    near = own + direct.astype(f32)

    state = (master, moment_first, moment_second)
    *state_new, row0, row1, row2, row3, extra = adam(
        place, changed, picked, (near, relay), state
    )

    extra = lax.ppermute(extra, ("dp", "mp"), SWAP)
    row = [row0] + [on_mp(r, along_x(s)) for s, r in ((1, row1), (2, row2), (3, row3))]
    plane, features = [], []
    for u in range(4):
        group = [r[128 * u : 128 * u + 128] for r in row + [extra]]
        group = jnp.concatenate(group + [r[512:] for r in row])
        if u:
            group = on_mp(group, along_y(u))
        plane.append(group[:640])
        features.append(group[640:])
    features = jnp.stack(features)
    mine = jnp.concatenate(plane).reshape(20, 128, 128)

    near = on_dp(mine, Z_WAY)
    paired = on_dp(mine, CORE)
    near_paired = on_dp(paired, Z_WAY)

    work, old = local(
        first_kernel,
        [SMEM, ANY, VMEM, VMEM],
        [VMEM] * 2,
        [SERVING, OLD],
        [pltpu.SemaphoreType.DMA(())],
    )(place, serving, mine, paired)
    near = tie(near, old)
    far = on_dp(near, Z_WAY)
    pieces = (near, on_dp(near, CORE), near_paired, on_dp(near_paired, CORE))
    _, out, total, features = local(
        second_kernel,
        [SMEM] + [VMEM] * 6,
        [VMEM, ANY, VMEM, VMEM],
        [SERVING, SERVING, TOTAL, FEATURES],
        [pltpu.SemaphoreType.DMA((8,))],
        {6: 0},
    )(place, features, *pieces, work)
    far = tie(far, total)
    serving_new, scores = local(
        last_kernel,
        [SMEM] + [VMEM] * 6 + [ANY],
        [ANY, VMEM],
        [SERVING, SCORES],
        [
            pltpu.VMEM(TOTAL.shape, f32),
            pltpu.VMEM(OLD.shape, bf16),
            pltpu.SemaphoreType.DMA((40,)),
        ],
        {7: 0},
    )(
        place,
        features,
        head_gain.reshape(1, 128),
        total,
        old,
        far,
        on_dp(far, CORE),
        out,
    )
    return (*state_new, serving_new, scores)


def solution(mesh):
    return jax.shard_map(
        on_device,
        mesh=mesh,
        in_specs=(
            P("dp", "mp", None, None),
            P(("mp", "dp"), None, None),
            P(("mp", "dp"), None, None),
            P(("mp", "dp"), None, None),
            P(None, "mp"),
            P(("mp", "dp")),
            P(None, "mp"),
            P("dp"),
            P(),
        ),
        out_specs=(
            P(("mp", "dp"), None, None),
            P(("mp", "dp"), None, None),
            P(("mp", "dp"), None, None),
            P(None, "mp"),
            P("dp", "mp"),
        ),
        check_vma=False,
    )
```

```python
import functools

import jax
import jax.numpy as jnp
from jax import lax
from jax.experimental import pallas as pl
from jax.experimental.pallas import tpu as pltpu
from jax.sharding import PartitionSpec as P

beta_one = 0.9
beta_two = 0.999
correct_one = 1.0 - (0.9**10) ** 10
correct_two = 1.0 - (0.999**10) ** 10
adam_eps = 1e-08
learn_rate = 0.001
weight_decay = 0.1

f32 = jnp.float32
bf16 = jnp.bfloat16
MiB = 1024 * 1024

Z_WAY = [(2 * z + c, 2 * ((z + 1 - 2 * c) % 4) + c) for z in range(4) for c in range(2)]
Z_BACK = [(2 * z + c, 2 * ((z + 3 + 2 * c) % 4) + c) for z in range(4) for c in range(2)]
CORE = [(i, i ^ 1) for i in range(8)]
SWAP = [
    (d * 16 + x * 4 + y, (d // 4 * 4 + x) * 16 + (d % 4) * 4 + y)
    for d in range(8)
    for x in range(4)
    for y in range(4)
]


def along_x(s):
    return [(x * 4 + y, (x + s) % 4 * 4 + y) for x in range(4) for y in range(4)]


def along_y(s):
    return [(x * 4 + y, x * 4 + (y + s) % 4) for x in range(4) for y in range(4)]


def on_dp(value, pairs):
    return lax.ppermute(value, "dp", pairs)


def on_mp(value, pairs):
    return lax.ppermute(value, "mp", pairs)


VMEM = pl.BlockSpec(memory_space=pltpu.VMEM)
SMEM = pl.BlockSpec(memory_space=pltpu.SMEM)
ANY = pl.BlockSpec(memory_space=pl.ANY)
BRIEF = pl.CostEstimate(flops=1000, bytes_accessed=1000, transcendentals=0)


def add(*terms):
    return sum(term.astype(f32) for term in terms).astype(bf16)


def tie(value, *earlier):
    return pl.pallas_call(
        lambda *refs: None,
        in_specs=[ANY] * (1 + len(earlier)),
        out_specs=ANY,
        out_shape=jax.ShapeDtypeStruct(value.shape, value.dtype),
        input_output_aliases={0: 0},
        compiler_params=pltpu.CompilerParams(vmem_limit_bytes=MiB),
        cost_estimate=BRIEF,
    )(value, *earlier)


def adam_kernel(place, marked, picked, near, relay, master, first, second, *refs):
    outs, slots = refs[:3], refs[3:]
    step = pl.program_id(0)
    x, y, e = place[1], place[2], place[3]
    to = jnp.where(step == 4, 4, (step + e - x + 4) % 4)
    for block in range(4):
        gradient = near[block] + relay[block].astype(f32)
        weight = master[block]
        first_new = beta_one * first[block] + (1.0 - beta_one) * gradient
        second_new = beta_two * second[block] + (1.0 - beta_two) * gradient * gradient
        update = (
            first_new / correct_one / (jnp.sqrt(second_new / correct_two) + adam_eps)
            + weight_decay * weight
        )
        weight_new = weight - learn_rate * update
        outs[0][block] = weight_new
        outs[1][block] = first_new
        outs[2][block] = second_new
        flag = marked[step * 4 + block]
        fresh = jnp.where(flag == 1, weight_new, jnp.inf).astype(bf16)
        rows = pl.ds(pl.multiple_of((block - y + 4) % 4 * 128, 128), 128)
        for number, slot in enumerate(slots):

            @pl.when(to == number)
            def _():
                slot[rows, :] = fresh

    @pl.when(step == 0)
    def _():
        for slot in slots[:4]:
            for j in range(3):
                slot[512 + 16 * j : 528 + 16 * j, :] = picked[:, 128 * j : 128 * j + 128]


def adam(place, changed, picked, terms, state):
    rows = pl.BlockSpec((4, 128, 128), lambda i, place, marked: (i, 0, 0))

    def whole(height, width):
        return pl.BlockSpec((height, width), lambda i, place, marked: (0, 0))

    heights = (560, 560, 560, 560, 512)
    return pl.pallas_call(
        adam_kernel,
        grid_spec=pltpu.PrefetchScalarGridSpec(
            num_scalar_prefetch=2,
            grid=(5,),
            in_specs=[whole(16, 384)] + [rows] * 5,
            out_specs=[rows] * 3 + [whole(height, 128) for height in heights],
        ),
        out_shape=[jax.ShapeDtypeStruct((20, 128, 128), f32)] * 3
        + [jax.ShapeDtypeStruct((height, 128), bf16) for height in heights],
        compiler_params=pltpu.CompilerParams(vmem_limit_bytes=16 * MiB),
        cost_estimate=BRIEF,
    )(place, changed, picked, *terms, *state)


def origin(place, steps, crossed, u, s):
    x, y, z, core = place[1], place[2], place[4], place[5]
    z_from = (z + steps * (1 - 2 * core) + 4) % 4
    e_from = 2 * (z_from % 2) + (core ^ crossed)
    y_from = (y - u + 4) % 4
    x_from = (x - s + 4) % 4
    late = (e_from > x).astype(jnp.int32)
    t = jnp.where(
        s < 4,
        10 * (4 * x_from + y_from) + e_from + late,
        10 * (4 * e_from + y_from) + x + 1,
    )
    t = t + 5 * (z_from // 2)
    return t // 4, t % 4


def blocks(place, where_from, pieces, body):
    for number, (piece, (steps, crossed)) in enumerate(zip(pieces, where_from)):

        def group(u, carry):
            for s in range(5):
                row, column = origin(place, steps, crossed, u, s)
                i = u * 5 + s
                body(number * 20 + i, None if piece is None else piece[i], row, column)
            return carry

        lax.fori_loop(0, 4, group, 0)


def spot(row, column):
    rows = pl.ds(pl.multiple_of(row * 128, 128), 128)
    return rows, pl.ds(pl.multiple_of(column * 128, 128), 128)


FIRST = ((0, 0), (0, 1))
SECOND = ((-1, 0), (1, 1), (-1, 1), (1, 0))
LAST = ((2, 0), (2, 1))


def first_kernel(place, serving, mine, paired, out, old, sem):
    copy = pltpu.make_async_copy(serving, out, sem)
    copy.start()
    copy.wait()

    def put(i, block, row, column):
        at = spot(row, column)
        out[at] = jnp.where(block == jnp.inf, out[at], block)

    def keep(i, block, row, column):
        at = spot(row, column)
        old[i] = out[at]
        out[at] = jnp.zeros((128, 128), bf16)

    blocks(place, FIRST, (mine, paired), put)
    blocks(place, LAST, (None, None), keep)


def second_kernel(place, picked, *refs):
    pieces, (_, work, out, total, features, sems) = refs[:4], refs[4:]
    features[...] = jnp.zeros((40, 16, 128), bf16)
    for u in range(4):
        for s in range(4):
            at = 4 * ((place[1] - s + 4) % 4) + (place[2] - u + 4) % 4
            tile = 5 * (at // 2) + 2 * (at % 2)
            for j in range(3):
                features[tile + j] += picked[u, pl.ds(s * 48 + j * 16, 16), :]

    def put(i, block, row, column):
        at = spot(row, column)
        work[at] = jnp.where(block == jnp.inf, work[at], block)

    def write(i):
        rows = pl.ds(i * 640, 640)
        return pltpu.make_async_copy(work.at[rows], out.at[rows], sems.at[i])

    blocks(place, SECOND, pieces, put)
    for i in range(8):
        write(i).start()
    query = jnp.zeros((16, 512), f32)
    for i in range(8):
        left = jnp.concatenate([features[5 * i + j] for j in range(5)], axis=1)
        query += jnp.dot(left, work[640 * i : 640 * i + 640, :], preferred_element_type=f32)
    for column in range(4):
        total[column] = query[:, column * 128 : column * 128 + 128]
    for i in range(8):
        write(i).wait()


def last_kernel(number, place, features, gain, before, old, piece, _, *refs):
    out, result, total, held, sems = refs
    total[...] = before[...]
    writes = []
    for odd in range(2):
        for wanted in ((0, 1, 2, 3), (4,)):
            first = len(writes)
            left = []
            for s in wanted:
                for u in (odd, odd + 2):
                    row, column = origin(place, *LAST[number], u, s)
                    i, n = u * 5 + s, len(writes)
                    block = piece[i]
                    held[n] = jnp.where(block == jnp.inf, old[number * 20 + i], block)
                    to = out.at[spot(row, column)]
                    writes.append(pltpu.make_async_copy(held.at[n], to, sems.at[n]))
                    writes[n].start()
                    left.append(features[row])
            right = held[first : len(writes)].reshape(-1, 128)
            left = jnp.concatenate(left, axis=1)
            total[column] += jnp.dot(left, right, preferred_element_type=f32)
    if number == 0:
        result[...] = total[...]
    else:
        for head in range(4):
            query = total[head]
            scale = lax.rsqrt(jnp.mean(query * query, axis=-1, keepdims=True) + 1e-06)
            columns = pl.ds(head * 128, 128)
            result[:, columns] = (query * scale * gain[...]).astype(bf16)
    for write in writes:
        write.wait()


SERVING = jax.ShapeDtypeStruct((5120, 512), bf16)
OLD = jax.ShapeDtypeStruct((40, 128, 128), bf16)
FEATURES = jax.ShapeDtypeStruct((40, 16, 128), bf16)
TOTAL = jax.ShapeDtypeStruct((4, 16, 128), f32)
SCORES = jax.ShapeDtypeStruct((16, 512), bf16)


def local(kernel, in_specs, out_specs, out_shape, scratch=(), aliases={}):
    return pl.pallas_call(
        kernel,
        in_specs=in_specs,
        out_specs=out_specs,
        out_shape=out_shape,
        scratch_shapes=scratch,
        input_output_aliases=aliases,
        compiler_params=pltpu.CompilerParams(vmem_limit_bytes=16 * MiB),
        cost_estimate=BRIEF,
    )


def on_device(
    grad_parts,
    master,
    moment_first,
    moment_second,
    serving,
    changed,
    hidden_pool,
    row_ids,
    head_gain,
):
    dp = lax.axis_index("dp")
    mp = lax.axis_index("mp")
    z, core = dp // 2, dp % 2
    x, y = mp // 4, mp % 4
    place = jnp.stack([dp, x, y, dp % 4, z, core]).astype(jnp.int32)

    other = 1 - core
    up = (z + 5 - 2 * core) % 4
    down = (z + 3 + 2 * core) % 4
    opposite = (z + 2) % 4

    picked = jnp.take(hidden_pool, row_ids, axis=0, mode="clip")
    even, odd = (jnp.pad(picked, ((0, 0), ends)) for ends in ((0, 64), (64, 0)))
    picked = jnp.where(y % 2 == 1, odd, even)

    parts = grad_parts.reshape(4, 2, 20, 128, 128)

    def part(chip, c, at=0, count=20):
        start = (chip, c, at, 0, 0)
        return lax.dynamic_slice(parts, start, (1, 1, count, 128, 128))[0, 0]

    def after(*values):
        nonlocal parts
        parts, *values = lax.optimization_barrier((parts, *values))
        return values

    far_out, far_keep = part(opposite, other), part(opposite, core)
    (far_out,) = after(far_out)
    direct_out, relay_out = part(up, other), part(down, other)
    (far,) = after(add(far_keep, on_dp(far_out, CORE)))
    far = on_dp(far, Z_WAY)
    (relay,) = after(add(part(up, core), on_dp(relay_out, CORE)))
    (own_out,) = after(part(z, other))
    direct_in = tie(on_dp(direct_out, CORE), relay, own_out)
    (direct,) = after(add(part(down, core), direct_in))
    far = tie(far, direct, picked)
    direct = on_dp(direct, Z_BACK)
    relay = on_dp(add(relay, far), Z_WAY)
    own = part(z, core).astype(f32) + on_dp(own_out, CORE).astype(f32)
    near = own + direct.astype(f32)

    state = (master, moment_first, moment_second)
    *state_new, row0, row1, row2, row3, extra = adam(
        place, changed, picked, (near, relay), state
    )

    extra = lax.ppermute(extra, ("dp", "mp"), SWAP)
    row = [row0] + [on_mp(r, along_x(s)) for s, r in ((1, row1), (2, row2), (3, row3))]
    plane, features = [], []
    for u in range(4):
        group = [r[128 * u : 128 * u + 128] for r in row + [extra]]
        group = jnp.concatenate(group + [r[512:] for r in row])
        if u:
            group = on_mp(group, along_y(u))
        plane.append(group[:640])
        features.append(group[640:])
    features = jnp.stack(features)
    mine = jnp.concatenate(plane).reshape(20, 128, 128)

    near = on_dp(mine, Z_WAY)
    paired = on_dp(mine, CORE)
    near_paired = on_dp(paired, Z_WAY)

    work, old = local(
        first_kernel,
        [SMEM, ANY, VMEM, VMEM],
        [VMEM] * 2,
        [SERVING, OLD],
        [pltpu.SemaphoreType.DMA(())],
    )(place, serving, mine, paired)
    near = tie(near, old)
    far = on_dp(near, Z_WAY)
    pieces = (near, on_dp(near, CORE), near_paired, on_dp(near_paired, CORE))
    _, out, total, features = local(
        second_kernel,
        [SMEM] + [VMEM] * 6,
        [VMEM, ANY, VMEM, VMEM],
        [SERVING, SERVING, TOTAL, FEATURES],
        [pltpu.SemaphoreType.DMA((8,))],
        {6: 0},
    )(place, features, *pieces, work)
    far = tie(far, total)
    gain = head_gain.reshape(1, 128)
    pieces = far, on_dp(far, CORE)
    for number, shape in enumerate((TOTAL, SCORES)):
        out, total = local(
            functools.partial(last_kernel, number),
            [SMEM] + [VMEM] * 5 + [ANY],
            [ANY, VMEM],
            [SERVING, shape],
            [
                pltpu.VMEM(TOTAL.shape, f32),
                pltpu.VMEM((20, 128, 128), bf16),
                pltpu.SemaphoreType.DMA((20,)),
            ],
            {6: 0},
        )(place, features, gain, total, old, pieces[number], out)
    return (*state_new, out, total)


def solution(mesh):
    return jax.shard_map(
        on_device,
        mesh=mesh,
        in_specs=(
            P("dp", "mp", None, None),
            P(("mp", "dp"), None, None),
            P(("mp", "dp"), None, None),
            P(("mp", "dp"), None, None),
            P(None, "mp"),
            P(("mp", "dp")),
            P(None, "mp"),
            P("dp"),
            P(),
        ),
        out_specs=(
            P(("mp", "dp"), None, None),
            P(("mp", "dp"), None, None),
            P(("mp", "dp"), None, None),
            P(None, "mp"),
            P("dp", "mp"),
        ),
        check_vma=False,
    )
```

```python
import functools

import jax
import jax.numpy as jnp
from jax import lax
from jax.experimental import pallas as pl
from jax.experimental.pallas import tpu as pltpu
from jax.sharding import PartitionSpec as P

beta_one = 0.9
beta_two = 0.999
correct_one = 1.0 - (0.9**10) ** 10
correct_two = 1.0 - (0.999**10) ** 10
adam_eps = 1e-08
learn_rate = 0.001
weight_decay = 0.1

f32 = jnp.float32
bf16 = jnp.bfloat16
MiB = 1024 * 1024

Z_WAY = [(2 * z + c, 2 * ((z + 1 - 2 * c) % 4) + c) for z in range(4) for c in range(2)]
Z_BACK = [(2 * z + c, 2 * ((z + 3 + 2 * c) % 4) + c) for z in range(4) for c in range(2)]
CORE = [(i, i ^ 1) for i in range(8)]
SWAP = [
    (d * 16 + x * 4 + y, (d // 4 * 4 + x) * 16 + (d % 4) * 4 + y)
    for d in range(8)
    for x in range(4)
    for y in range(4)
]


def along_x(s):
    return [(x * 4 + y, (x + s) % 4 * 4 + y) for x in range(4) for y in range(4)]


def along_y(s):
    return [(x * 4 + y, x * 4 + (y + s) % 4) for x in range(4) for y in range(4)]


def on_dp(value, pairs):
    return lax.ppermute(value, "dp", pairs)


def on_mp(value, pairs):
    return lax.ppermute(value, "mp", pairs)


VMEM = pl.BlockSpec(memory_space=pltpu.VMEM)
SMEM = pl.BlockSpec(memory_space=pltpu.SMEM)
ANY = pl.BlockSpec(memory_space=pl.ANY)
BRIEF = pl.CostEstimate(flops=1000, bytes_accessed=1000, transcendentals=0)


def add(*terms):
    return sum(term.astype(f32) for term in terms).astype(bf16)


def tie(value, *earlier):
    return pl.pallas_call(
        lambda *refs: None,
        in_specs=[ANY] * (1 + len(earlier)),
        out_specs=ANY,
        out_shape=jax.ShapeDtypeStruct(value.shape, value.dtype),
        input_output_aliases={0: 0},
        compiler_params=pltpu.CompilerParams(vmem_limit_bytes=MiB),
        cost_estimate=BRIEF,
    )(value, *earlier)


def adam_kernel(place, marked, picked, near, relay, master, first, second, *refs):
    outs, slots = refs[:3], refs[3:]
    step = pl.program_id(0)
    x, y, e = place[1], place[2], place[3]
    to = jnp.where(step == 4, 4, (step + e - x + 4) % 4)
    for block in range(4):
        gradient = near[block] + relay[block].astype(f32)
        weight = master[block]
        first_new = beta_one * first[block] + (1.0 - beta_one) * gradient
        second_new = beta_two * second[block] + (1.0 - beta_two) * gradient * gradient
        update = (
            first_new / correct_one / (jnp.sqrt(second_new / correct_two) + adam_eps)
            + weight_decay * weight
        )
        weight_new = weight - learn_rate * update
        outs[0][block] = weight_new
        outs[1][block] = first_new
        outs[2][block] = second_new
        flag = marked[step * 4 + block]
        fresh = jnp.where(flag == 1, weight_new, jnp.inf).astype(bf16)
        rows = pl.ds(pl.multiple_of((block - y + 4) % 4 * 128, 128), 128)
        for number, slot in enumerate(slots):

            @pl.when(to == number)
            def _():
                slot[rows, :] = fresh

    @pl.when(step == 0)
    def _():
        for slot in slots[:4]:
            for j in range(3):
                slot[512 + 16 * j : 528 + 16 * j, :] = picked[:, 128 * j : 128 * j + 128]


def adam(place, changed, picked, terms, state):
    rows = pl.BlockSpec((4, 128, 128), lambda i, place, marked: (i, 0, 0))

    def whole(height, width):
        return pl.BlockSpec((height, width), lambda i, place, marked: (0, 0))

    heights = (560, 560, 560, 560, 512)
    return pl.pallas_call(
        adam_kernel,
        grid_spec=pltpu.PrefetchScalarGridSpec(
            num_scalar_prefetch=2,
            grid=(5,),
            in_specs=[whole(16, 384)] + [rows] * 5,
            out_specs=[rows] * 3 + [whole(height, 128) for height in heights],
        ),
        out_shape=[jax.ShapeDtypeStruct((20, 128, 128), f32)] * 3
        + [jax.ShapeDtypeStruct((height, 128), bf16) for height in heights],
        compiler_params=pltpu.CompilerParams(vmem_limit_bytes=16 * MiB),
        cost_estimate=BRIEF,
    )(place, changed, picked, *terms, *state)


def origin(place, steps, crossed, u, s):
    x, y, z, core = place[1], place[2], place[4], place[5]
    z_from = (z + steps * (1 - 2 * core) + 4) % 4
    e_from = 2 * (z_from % 2) + (core ^ crossed)
    y_from = (y - u + 4) % 4
    x_from = (x - s + 4) % 4
    late = (e_from > x).astype(jnp.int32)
    t = jnp.where(
        s < 4,
        10 * (4 * x_from + y_from) + e_from + late,
        10 * (4 * e_from + y_from) + x + 1,
    )
    t = t + 5 * (z_from // 2)
    return t // 4, t % 4


def blocks(place, where_from, pieces, body):
    for number, (piece, (steps, crossed)) in enumerate(zip(pieces, where_from)):

        def group(u, carry):
            for s in range(5):
                row, column = origin(place, steps, crossed, u, s)
                i = u * 5 + s
                body(number * 20 + i, None if piece is None else piece[i], row, column)
            return carry

        lax.fori_loop(0, 4, group, 0)


def spot(row, column):
    rows = pl.ds(pl.multiple_of(row * 128, 128), 128)
    return rows, pl.ds(pl.multiple_of(column * 128, 128), 128)


FIRST = ((0, 0), (0, 1))
SECOND = ((-1, 0), (1, 1), (-1, 1), (1, 0))
LAST = ((2, 0), (2, 1))


def first_kernel(place, serving, mine, paired, out, old, sem):
    copy = pltpu.make_async_copy(serving, out, sem)
    copy.start()
    copy.wait()

    def put(i, block, row, column):
        at = spot(row, column)
        out[at] = jnp.where(block == jnp.inf, out[at], block)

    def keep(i, block, row, column):
        at = spot(row, column)
        old[i] = out[at]
        out[at] = jnp.zeros((128, 128), bf16)

    blocks(place, FIRST, (mine, paired), put)
    blocks(place, LAST, (None, None), keep)


def second_kernel(place, picked, *refs):
    pieces, (_, work, out, total, features, sems) = refs[:4], refs[4:]
    features[...] = jnp.zeros((40, 16, 128), bf16)
    for u in range(4):
        for s in range(4):
            at = 4 * ((place[1] - s + 4) % 4) + (place[2] - u + 4) % 4
            tile = 5 * (at // 2) + 2 * (at % 2)
            for j in range(3):
                features[tile + j] += picked[u, pl.ds(s * 48 + j * 16, 16), :]

    def put(i, block, row, column):
        at = spot(row, column)
        work[at] = jnp.where(block == jnp.inf, work[at], block)

    def write(i):
        rows = pl.ds(i * 640, 640)
        return pltpu.make_async_copy(work.at[rows], out.at[rows], sems.at[i])

    blocks(place, SECOND, pieces, put)
    for i in range(8):
        write(i).start()
    query = jnp.zeros((16, 512), f32)
    for i in range(8):
        left = jnp.concatenate([features[5 * i + j] for j in range(5)], axis=1)
        query += jnp.dot(left, work[640 * i : 640 * i + 640, :], preferred_element_type=f32)
    for column in range(4):
        total[column] = query[:, column * 128 : column * 128 + 128]
    for i in range(8):
        write(i).wait()


def last_kernel(number, place, features, gain, before, old, piece, _, *refs):
    out, result, total, held, sems = refs
    total[...] = before[...]
    writes = []
    for odd in range(2):
        for wanted in ((0, 1, 2, 3), (4,)):
            first = len(writes)
            left = []
            for s in wanted:
                for u in (odd, odd + 2):
                    row, column = origin(place, *LAST[number], u, s)
                    i, n = u * 5 + s, len(writes)
                    block = piece[i]
                    held[n] = jnp.where(block == jnp.inf, old[number * 20 + i], block)
                    to = out.at[spot(row, column)]
                    writes.append(pltpu.make_async_copy(held.at[n], to, sems.at[n]))
                    writes[n].start()
                    left.append(features[row])
            right = held[first : len(writes)].reshape(-1, 128)
            left = jnp.concatenate(left, axis=1)
            total[column] += jnp.dot(left, right, preferred_element_type=f32)
    if number == 0:
        result[...] = total[...]
    else:
        for head in range(4):
            query = total[head]
            scale = lax.rsqrt(jnp.mean(query * query, axis=-1, keepdims=True) + 1e-06)
            columns = pl.ds(head * 128, 128)
            result[:, columns] = (query * scale * gain[...]).astype(bf16)
    for write in writes:
        write.wait()


SERVING = jax.ShapeDtypeStruct((5120, 512), bf16)
OLD = jax.ShapeDtypeStruct((40, 128, 128), bf16)
FEATURES = jax.ShapeDtypeStruct((40, 16, 128), bf16)
TOTAL = jax.ShapeDtypeStruct((4, 16, 128), f32)
SCORES = jax.ShapeDtypeStruct((16, 512), bf16)


def local(kernel, in_specs, out_specs, out_shape, scratch=(), aliases={}):
    return pl.pallas_call(
        kernel,
        in_specs=in_specs,
        out_specs=out_specs,
        out_shape=out_shape,
        scratch_shapes=scratch,
        input_output_aliases=aliases,
        compiler_params=pltpu.CompilerParams(vmem_limit_bytes=16 * MiB),
        cost_estimate=BRIEF,
    )


def on_device(
    grad_parts,
    master,
    moment_first,
    moment_second,
    serving,
    changed,
    hidden_pool,
    row_ids,
    head_gain,
):
    dp = lax.axis_index("dp")
    mp = lax.axis_index("mp")
    z, core = dp // 2, dp % 2
    x, y = mp // 4, mp % 4
    place = jnp.stack([dp, x, y, dp % 4, z, core]).astype(jnp.int32)

    other = 1 - core
    up = (z + 5 - 2 * core) % 4
    down = (z + 3 + 2 * core) % 4
    opposite = (z + 2) % 4

    pool = jnp.arange(hidden_pool.shape[0], dtype=jnp.int32)
    chosen = (row_ids[:, None] == pool[None, :]).astype(bf16)
    picked = jnp.dot(chosen, hidden_pool, preferred_element_type=f32).astype(bf16)
    even, odd = (jnp.pad(picked, ((0, 0), ends)) for ends in ((0, 64), (64, 0)))
    picked = jnp.where(y % 2 == 1, odd, even)

    parts = grad_parts.reshape(4, 2, 20, 128, 128)

    def part(chip, c, at=0, count=20):
        start = (chip, c, at, 0, 0)
        return lax.dynamic_slice(parts, start, (1, 1, count, 128, 128))[0, 0]

    def after(*values):
        nonlocal parts
        parts, *values = lax.optimization_barrier((parts, *values))
        return values

    far_out, far_keep = part(opposite, other), part(opposite, core)
    (far_out,) = after(far_out)
    direct_out, relay_out = part(up, other), part(down, other)
    (far,) = after(add(far_keep, on_dp(far_out, CORE)))
    far = on_dp(far, Z_WAY)
    (relay,) = after(add(part(up, core), on_dp(relay_out, CORE)))
    (own_out,) = after(part(z, other))
    direct_in = tie(on_dp(direct_out, CORE), relay, own_out)
    (direct,) = after(add(part(down, core), direct_in))
    far = tie(far, direct, picked)
    direct = on_dp(direct, Z_BACK)
    relay = on_dp(add(relay, far), Z_WAY)
    own = part(z, core).astype(f32) + on_dp(own_out, CORE).astype(f32)
    near = own + direct.astype(f32)

    state = (master, moment_first, moment_second)
    *state_new, row0, row1, row2, row3, extra = adam(
        place, changed, picked, (near, relay), state
    )

    extra = lax.ppermute(extra, ("dp", "mp"), SWAP)
    row = [row0] + [on_mp(r, along_x(s)) for s, r in ((1, row1), (2, row2), (3, row3))]
    plane, features = [], []
    for u in range(4):
        group = [r[128 * u : 128 * u + 128] for r in row + [extra]]
        group = jnp.concatenate(group + [r[512:] for r in row])
        if u:
            group = on_mp(group, along_y(u))
        plane.append(group[:640])
        features.append(group[640:])
    features = jnp.stack(features)
    mine = jnp.concatenate(plane).reshape(20, 128, 128)

    near = on_dp(mine, Z_WAY)
    paired = on_dp(mine, CORE)
    near_paired = on_dp(paired, Z_WAY)

    work, old = local(
        first_kernel,
        [SMEM, ANY, VMEM, VMEM],
        [VMEM] * 2,
        [SERVING, OLD],
        [pltpu.SemaphoreType.DMA(())],
    )(place, serving, mine, paired)
    near = tie(near, old)
    far = on_dp(near, Z_WAY)
    pieces = (near, on_dp(near, CORE), near_paired, on_dp(near_paired, CORE))
    _, out, total, features = local(
        second_kernel,
        [SMEM] + [VMEM] * 6,
        [VMEM, ANY, VMEM, VMEM],
        [SERVING, SERVING, TOTAL, FEATURES],
        [pltpu.SemaphoreType.DMA((8,))],
        {6: 0},
    )(place, features, *pieces, work)
    far = tie(far, total)
    gain = head_gain.reshape(1, 128)
    pieces = far, on_dp(far, CORE)
    for number, shape in enumerate((TOTAL, SCORES)):
        out, total = local(
            functools.partial(last_kernel, number),
            [SMEM] + [VMEM] * 5 + [ANY],
            [ANY, VMEM],
            [SERVING, shape],
            [
                pltpu.VMEM(TOTAL.shape, f32),
                pltpu.VMEM((20, 128, 128), bf16),
                pltpu.SemaphoreType.DMA((20,)),
            ],
            {6: 0},
        )(place, features, gain, total, old, pieces[number], out)
    return (*state_new, out, total)


def solution(mesh):
    return jax.shard_map(
        on_device,
        mesh=mesh,
        in_specs=(
            P("dp", "mp", None, None),
            P(("mp", "dp"), None, None),
            P(("mp", "dp"), None, None),
            P(("mp", "dp"), None, None),
            P(None, "mp"),
            P(("mp", "dp")),
            P(None, "mp"),
            P("dp"),
            P(),
        ),
        out_specs=(
            P(("mp", "dp"), None, None),
            P(("mp", "dp"), None, None),
            P(("mp", "dp"), None, None),
            P(None, "mp"),
            P("dp", "mp"),
        ),
        check_vma=False,
    )
```
